256 devices in a mesh: rows: 32 (over x, z_hi, core), feat: 8 (over y, z_lo).
Axes of the slice: x: 4, y: 4, z: 8 (z_hi: 4, z_lo: 2; z = z_hi * 2 + z_lo), core: 2. Of those that a mesh axis runs over, the one named last changes fastest.
Arguments:
- data: bfloat16 [196608, 1024], P(('rows', 'feat')), may hold values from -6 to 6
- rotation: bfloat16 [1024, 1024], P(None, 'feat'), may hold values from -0.1875 to 0.1875
- codebook: bfloat16 [256, 1024], P(None, 'feat'), may hold values from -5 to 5
Outputs:
- new_codebook: float32 [256, 1024], P(None, 'feat')
- counts: float32 [64, 256], P('feat')
- cross: float32 [1024, 1024], P('rows', 'feat')
The draws below stay inside these ranges and needn't reach their ends.
All inputs are finite; a program needn't handle non-finite values.
Results may differ from the reference program's by a relative error of at most 0.0029.
Values may be sent and summed in bfloat16 or wider, within the bound.
No kernel may reach another device: no remote copies, remote signals or barrier semaphores. Data moves between devices by JAX's collectives and lax.ppermute only.
A program may use at most 64 MiB of HBM per device.

```python
import jax
import jax.numpy as jnp
from jax import lax

D = 1024
SUB = 64
K = 256
ROWS_ALL = 196608


def draw_codebook(key, part):
    values = jnp.clip(jax.random.normal(key, (K, D), jnp.float32), -4.0, 4.0)
    return values.astype(jnp.bfloat16)


def shard_levels(key, shape, cuts, smallest, top_value):
    level = 1.0
    for position, blocks in cuts:
        steps = jax.random.uniform(jax.random.fold_in(jax.random.fold_in(key, 6), position), (blocks,), jnp.float32, smallest / len(cuts), top_value / len(cuts))
        level = level * jnp.repeat(jnp.exp(steps), shape[position] // blocks).reshape((-1,) + (1,) * (len(shape) - 1 - position))
    return level


def noise(own_key, dims, scale, limit, cuts=(), held_as=jnp.bfloat16):
    loudness = shard_levels(own_key, dims, cuts, -0.22, 0.18) if cuts else 1.0
    entries = jax.random.normal(own_key, dims, jnp.float32) * scale * loudness
    return jnp.minimum(jnp.maximum(entries, -limit), limit).astype(held_as)


def setup_inputs(seed: int = 0) -> dict:
    key_of = jax.random.split(jax.random.key(seed), 4)
    return {
        "data": noise(key_of[0], (ROWS_ALL, D), 1.0, 6.0, ((0, 256),)),
        "rotation": noise(key_of[1], (D, D), D ** -0.5, 0.1875, ((1, 8),)),
        "codebook": draw_codebook(jax.random.fold_in(key_of[3], 71), 0),
    }


inverse_temp = 0.5


def assign_block(piece, codebook):
    width = D // SUB
    rows_here = piece.shape[0]
    values = piece.astype(jnp.float32).reshape(rows_here, SUB, width)
    codes = codebook.astype(jnp.float32).reshape(K, SUB, width)
    dots = jnp.einsum("nsd,ksd->snk", values, codes)
    squares = jnp.sum(codes * codes, axis=-1).T[:, None, :]
    logits = inverse_temp * (2.0 * dots - squares)
    weights = jax.nn.softmax(logits, axis=-1)
    weights_b = weights.astype(jnp.bfloat16).astype(jnp.float32)
    numer = jnp.einsum("snk,nsd->ksd", weights_b, values).reshape(K, D)
    counted = jnp.sum(weights, axis=1)
    rebuilt = jnp.einsum("snk,ksd->nsd", weights_b, codes).reshape(rows_here, D).astype(jnp.bfloat16)
    return numer, counted, rebuilt


def reference(data, rotation, codebook):
    total_rows = data.shape[0]
    rotated = jnp.dot(data, rotation, preferred_element_type=jnp.float32).astype(jnp.bfloat16)
    block = 4096 if total_rows % 4096 == 0 else total_rows
    pieces = rotated.reshape(total_rows // block, block, D)

    def step(carry, piece):
        numer, counted = carry
        add_numer, add_counts, rebuilt = assign_block(piece, codebook)
        return (numer + add_numer, counted + add_counts), rebuilt

    start = (jnp.zeros((K, D), jnp.float32), jnp.zeros((SUB, K), jnp.float32))
    (numer, counted), rebuilt = lax.scan(step, start, pieces)
    rebuilt = rebuilt.reshape(total_rows, D)
    per_column = jnp.repeat(counted.T, D // SUB, axis=1)
    new_codebook = (numer + codebook.astype(jnp.float32)) / (per_column + 1.0)
    cross = jnp.dot(data.T, rebuilt, preferred_element_type=jnp.float32)
    return new_codebook, counted, cross
```

```python
import jax
import jax.numpy as jnp
from jax import lax
from jax.experimental import pallas as pl
from jax.experimental.pallas import tpu as pltpu
from jax.sharding import PartitionSpec as P

D = 1024
SUB = 64
K = 256
SW = D // SUB
W = 128
NS = W // SW
ROWS = 768
CHUNK = 256
HALF = D // 2 + K // 2 + NS
bf16 = jnp.bfloat16
f32 = jnp.float32


def dot(a, b, ca, cb):
    return lax.dot_general(a, b, (((ca,), (cb,)), ((), ())), preferred_element_type=f32)


def assign_kernel(data_ref, pack_ref, out_ref, xaug, reb, wb):
    codes_t = pack_ref[0, :, D:]
    codes = codes_t.astype(f32).T.astype(bf16)
    wide = codes.astype(f32)
    squares = wide * wide
    high = squares.astype(bf16)
    low = (squares - high.astype(f32)).astype(bf16)
    row_group = lax.broadcasted_iota(jnp.int32, (W, W), 0) // SW
    col_group = lax.broadcasted_iota(jnp.int32, (W, W), 1) // SW
    group_ones = jnp.where(row_group == col_group, 1.0, 0.0).astype(bf16)
    bias = -0.5 * (dot(high, group_ones, 1, 0) + dot(low, group_ones, 1, 0))
    lane = lax.broadcasted_iota(jnp.int32, (K, W), 1)
    b0 = bias.astype(bf16).astype(f32)
    b1 = (bias - b0).astype(bf16).astype(f32)
    b2 = bias - b0 - b1
    place = lane % SW
    aug = jnp.where(place == 0, b0, jnp.where(place == 1, b1, jnp.where(place == 2, b2, 0.0))).astype(bf16)
    xaug[0:W, :] = dot(pack_ref[0, :, :D], data_ref[...], 1, 0).astype(bf16)
    xaug[W:, :] = jnp.ones((W, ROWS), bf16)
    acc = jnp.zeros((K, 2 * W), f32)
    group2 = (lax.broadcasted_iota(jnp.int32, (K, 2 * W), 1) // SW) % NS
    zero = jnp.zeros((K, W), bf16)
    for s in range(NS):
        mask = (lane // SW) == s
        lhs = jnp.concatenate([jnp.where(mask, codes, zero), jnp.where(mask, aug, zero)], axis=1)
        for piece in range(ROWS // CHUNK):
            cols = slice(piece * CHUNK, (piece + 1) * CHUNK)
            logits = dot(lhs, xaug[:, cols], 1, 0)
            e = jnp.exp(logits - jnp.max(logits, axis=0, keepdims=True))
            wb[:, cols] = (e * (1.0 / jnp.sum(e, axis=0, keepdims=True))).astype(bf16)
        own = slice(s * SW, (s + 1) * SW)
        reb[own, :] = dot(pack_ref[0, own, D:], wb[...], 1, 0).astype(bf16)
        acc = jnp.where(group2 == s, dot(wb[...], xaug[...], 1, 1), acc)
    counts = acc[:, W:].T
    counts = jnp.concatenate([counts[s * SW : s * SW + 1] for s in range(NS)], axis=0)
    cross = dot(data_ref[...], reb[...], 1, 1)
    for h in range(2):
        out_ref[0, h, : D // 2, :] = cross[h * (D // 2) : (h + 1) * (D // 2)]
        out_ref[0, h, D // 2 : D // 2 + K // 2, :] = acc[h * (K // 2) : (h + 1) * (K // 2), :W]
        out_ref[0, h, D // 2 + K // 2 :, :] = counts[:, h * (K // 2) : (h + 1) * (K // 2)]


def assign(data_t, packs):
    blocks = packs.shape[0]
    return pl.pallas_call(
        assign_kernel,
        grid=(blocks,),
        in_specs=[
            pl.BlockSpec((D, ROWS), lambda g: (0, 0)),
            pl.BlockSpec((1, W, D + K), lambda g: (g, 0, 0)),
        ],
        out_specs=pl.BlockSpec((1, 2, HALF, W), lambda g: (g, 0, 0, 0)),
        out_shape=jax.ShapeDtypeStruct((blocks, 2, HALF, W), f32),
        scratch_shapes=[
            pltpu.VMEM((2 * W, ROWS), bf16),
            pltpu.VMEM((W, ROWS), bf16),
            pltpu.VMEM((K, ROWS), bf16),
        ],
        compiler_params=pltpu.CompilerParams(vmem_limit_bytes=48 * 1024 * 1024),
        name="assign",
    )(data_t, packs)


def local(data, rotation, codebook):
    n_feat = lax.axis_size("feat")
    n_rows = lax.axis_size("rows")
    pairs = n_rows // 2
    core = lax.axis_index("rows") % 2
    swap = [(i, i ^ 1) for i in range(n_rows)]
    lanes = D // n_rows
    data_t = data.reshape(ROWS, pairs, 2, lanes).transpose(2, 1, 3, 0).reshape(D, ROWS)
    rot_t = rotation.reshape(pairs, 2, lanes, W).transpose(3, 1, 0, 2).reshape(W, D)
    pack = jnp.concatenate([rot_t, codebook.T], axis=1)
    half = lax.dynamic_slice_in_dim(pack, core * (W // 2), W // 2, axis=0)
    mine = lax.all_to_all(
        jnp.broadcast_to(half[None], (n_feat,) + half.shape), "feat", split_axis=0, concat_axis=0, tiled=True
    )
    other = lax.ppermute(mine, "rows", swap)
    first = core == 0
    packs = jnp.concatenate([jnp.where(first, mine, other), jnp.where(first, other, mine)], axis=1)
    out = assign(data_t, packs)
    give = lax.dynamic_index_in_dim(out, 1 - core, axis=1, keepdims=False)
    keep = lax.dynamic_index_in_dim(out, core, axis=1, keepdims=False)
    summed = (keep + lax.ppermute(give, "rows", swap)).astype(LINK)
    got = lax.all_to_all(summed, "feat", split_axis=0, concat_axis=0, tiled=True)
    part = jnp.sum(got.astype(f32), axis=0)
    groups = [[i * 2 + c for i in range(pairs)] for c in range(2)]
    cross_part = part[: D // 2].reshape(pairs, lanes, W)
    numer_part = part[D // 2 : D // 2 + K // 2].reshape(pairs, K // n_rows, W)
    count_part = jnp.broadcast_to(part[D // 2 + K // 2 :][None], (pairs, NS, W))
    sent = jnp.concatenate([cross_part, numer_part, count_part], axis=1)
    total = jnp.sum(
        lax.all_to_all(sent, "rows", split_axis=0, concat_axis=0, tiled=True, axis_index_groups=groups), axis=0
    )
    cross = total[:lanes]
    tail = total[lanes:]
    whole = lax.all_to_all(
        jnp.broadcast_to(tail[None], (n_rows,) + tail.shape), "rows", split_axis=0, concat_axis=0, tiled=True
    )
    k_rows = K // n_rows
    numer = whole[:, :k_rows].reshape(pairs, 2, k_rows, W).transpose(1, 0, 2, 3).reshape(K, W)
    counts = whole[:2, k_rows:].transpose(1, 0, 2).reshape(NS, K)
    per_column = jnp.repeat(counts.T, SW, axis=1)
    new_codebook = (numer + codebook.astype(f32)) / (per_column + 1.0)
    return new_codebook, counts, cross


LINK = bf16


def solution(mesh):
    in_specs = (P(("rows", "feat"), None), P(None, "feat"), P(None, "feat"))
    out_specs = (P(None, "feat"), P("feat", None), P("rows", "feat"))
    return jax.shard_map(local, mesh=mesh, in_specs=in_specs, out_specs=out_specs, check_vma=False)
```

```python
import jax
import jax.numpy as jnp
from jax import lax
from jax.experimental import pallas as pl
from jax.experimental.pallas import tpu as pltpu
from jax.sharding import PartitionSpec as P

D = 1024
SUB = 64
K = 256
SW = D // SUB
W = 128
NS = W // SW
ROWS = 768
CHUNK = 256
CROSS = D // 2
NUMER = K // 2
HALF = CROSS + NUMER + NS
STEPS = ((1,), (2,), (3,), (4,), (5,), (6,), (7,), (0,))
LAG_SWAP = 99
LAG_SEND = 99
bf16 = jnp.bfloat16
f32 = jnp.float32


def dot(a, b, ca, cb):
    return lax.dot_general(a, b, (((ca,), (cb,)), ((), ())), preferred_element_type=f32)


def one_block(first, data_ref, mine, other, keep_ref, give_ref, codes_t, xaug, reb, wb, lhs_all):
    lo = jnp.where(first, mine[...], other[...])
    hi = jnp.where(first, other[...], mine[...])
    codes_t[0 : W // 2] = lo[:, D:]
    codes_t[W // 2 :] = hi[:, D:]
    codes = codes_t[...].astype(f32).T.astype(bf16)
    wide = codes.astype(f32)
    squares = wide * wide
    high = squares.astype(bf16)
    low = (squares - high.astype(f32)).astype(bf16)
    row_group = lax.broadcasted_iota(jnp.int32, (W, W), 0) // SW
    col_group = lax.broadcasted_iota(jnp.int32, (W, W), 1) // SW
    group_ones = jnp.where(row_group == col_group, 1.0, 0.0).astype(bf16)
    bias = -0.5 * (dot(high, group_ones, 1, 0) + dot(low, group_ones, 1, 0))
    lane = lax.broadcasted_iota(jnp.int32, (K, W), 1)
    b0 = bias.astype(bf16).astype(f32)
    b1 = (bias - b0).astype(bf16).astype(f32)
    b2 = bias - b0 - b1
    place = lane % SW
    aug = jnp.where(place == 0, b0, jnp.where(place == 1, b1, jnp.where(place == 2, b2, 0.0))).astype(bf16)
    rot = jnp.concatenate([lo[:, :D], hi[:, :D]], axis=0)
    xaug[0:W, :] = dot(rot, data_ref[...], 1, 0).astype(bf16)
    xaug[W:, :] = jnp.ones((W, ROWS), bf16)
    zero = jnp.zeros((K, W), bf16)
    for s in range(NS):
        mask = (lane // SW) == s
        lhs_all[s * K : (s + 1) * K, :] = jnp.concatenate(
            [jnp.where(mask, codes, zero), jnp.where(mask, aug, zero)], axis=1
        )
    for s in range(NS):
        for piece in range(ROWS // CHUNK):
            cols = slice(piece * CHUNK, (piece + 1) * CHUNK)
            logits = dot(lhs_all[s * K : (s + 1) * K, :], xaug[:, cols], 1, 0)
            e = jnp.exp(logits - jnp.max(logits, axis=0, keepdims=True))
            wb[s * K : (s + 1) * K, cols] = (e * (1.0 / jnp.sum(e, axis=0, keepdims=True))).astype(bf16)
    acc = jnp.zeros((K, 2 * W), f32)
    group2 = (lax.broadcasted_iota(jnp.int32, (K, 2 * W), 1) // SW) % NS
    for s in range(NS):
        own = slice(s * SW, (s + 1) * SW)
        weights = wb[s * K : (s + 1) * K, :]
        reb[own, :] = dot(codes_t[own, :], weights, 1, 0).astype(bf16)
        acc = jnp.where(group2 == s, dot(weights, xaug[...], 1, 1), acc)
    counts = acc[:, W:].T
    counts = jnp.concatenate([counts[s * SW : s * SW + 1] for s in range(NS)], axis=0)
    cross = dot(data_ref[...], reb[...], 1, 1)
    for ref, top in ((keep_ref, first), (give_ref, jnp.logical_not(first))):
        ref[:CROSS, :] = jnp.where(top, cross[:CROSS], cross[CROSS:])
        ref[CROSS : CROSS + NUMER, :] = jnp.where(top, acc[:NUMER, :W], acc[NUMER:, :W])
        ref[CROSS + NUMER :, :] = jnp.where(top, counts[:, :NUMER], counts[:, NUMER:])


def assign(core, data_t, packs):
    blocks = len(packs)

    def body(core_ref, data_ref, *refs):
        ins = refs[: 2 * blocks]
        outs = refs[2 * blocks : 4 * blocks]
        scratch = refs[4 * blocks :]
        first = core_ref[0] == 0
        for b in range(blocks):
            one_block(first, data_ref, ins[2 * b], ins[2 * b + 1], outs[2 * b], outs[2 * b + 1], *scratch)

    vmem = pl.BlockSpec(memory_space=pltpu.VMEM)
    flat = [half for pair in packs for half in pair]
    out = pl.pallas_call(
        body,
        in_specs=[pl.BlockSpec(memory_space=pltpu.SMEM), vmem] + [vmem] * len(flat),
        out_specs=[vmem] * (2 * blocks),
        out_shape=[jax.ShapeDtypeStruct((HALF, W), f32)] * (2 * blocks),
        scratch_shapes=[
            pltpu.VMEM((W, K), bf16),
            pltpu.VMEM((2 * W, ROWS), bf16),
            pltpu.VMEM((W, ROWS), bf16),
            pltpu.VMEM((NS * K, ROWS), bf16),
            pltpu.VMEM((NS * K, 2 * W), bf16),
        ],
        compiler_params=pltpu.CompilerParams(vmem_limit_bytes=24 * 1024 * 1024),
        cost_estimate=pl.CostEstimate(
            flops=blocks * 3_000_000_000, bytes_accessed=blocks * 4_000_000, transcendentals=blocks * NS * K * ROWS
        ),
        name="assign",
    )(core.reshape(1), data_t, *flat)
    return [(out[2 * b], out[2 * b + 1]) for b in range(blocks)]


def send(j, summed):
    n_feat = lax.axis_size("feat")
    return lax.ppermute(summed, "feat", [(i, (i + j) % n_feat) for i in range(n_feat)])


def local(data, rotation, codebook):
    n_feat = lax.axis_size("feat")
    n_rows = lax.axis_size("rows")
    pairs = n_rows // 2
    core = lax.axis_index("rows") % 2
    swap = [(i, i ^ 1) for i in range(n_rows)]
    lanes = D // n_rows
    rot_t = rotation.reshape(pairs, 2, lanes, W).transpose(3, 1, 0, 2).reshape(W, D)
    pack = jnp.concatenate([rot_t, codebook.T], axis=1)
    half = lax.dynamic_slice_in_dim(pack, core * (W // 2), W // 2, axis=0)
    other_half = lax.dynamic_slice_in_dim(pack, (1 - core) * (W // 2), W // 2, axis=0)
    data_t = data.reshape(ROWS, pairs, 2, lanes).transpose(2, 1, 3, 0).reshape(D, ROWS)
    packs = {0: (half, other_half)}
    for step in STEPS:
        for j in step:
            if j:
                mine = lax.ppermute(half, "feat", [(i, (i - j) % n_feat) for i in range(n_feat)])
                packs[j] = (mine, lax.ppermute(mine, "rows", swap))
    part = None
    waiting = []
    swapped = []
    for step in STEPS:
        ins = [packs[j] for j in step]
        if len(swapped) >= LAG_SWAP:
            j, summed = swapped.pop(0)
            ins, summed = lax.optimization_barrier((ins, summed))
            waiting.append((j, send(j, summed)))
        if len(waiting) >= LAG_SEND:
            j, got = waiting.pop(0)
            ins, got = lax.optimization_barrier((ins, got))
            part = got.astype(f32) if part is None else part + got.astype(f32)
        results = assign(core, data_t, ins)
        for j, (keep, give) in zip(step, results):
            summed = keep + lax.ppermute(give, "rows", swap)
            if j:
                swapped.append((j, summed.astype(bf16)))
            else:
                own = summed
    waiting += [(j, send(j, summed)) for j, summed in swapped]
    for j, got in waiting:
        part = got.astype(f32) if part is None else part + got.astype(f32)
    part = part + own
    groups = [[i * 2 + c for i in range(pairs)] for c in range(2)]
    rest = part[CROSS:]
    rest_high = rest.astype(bf16)
    counts_low = (rest[NUMER:] - rest_high[NUMER:].astype(f32)).astype(bf16)
    all_rest = jnp.concatenate([rest_high, counts_low], axis=0)
    sent = jnp.concatenate(
        [
            part[:CROSS].astype(bf16).reshape(pairs, lanes, W),
            jnp.broadcast_to(all_rest[None], (pairs,) + all_rest.shape),
        ],
        axis=1,
    )
    got = lax.all_to_all(sent, "rows", split_axis=0, concat_axis=0, tiled=True, axis_index_groups=groups)
    total = jnp.sum(got.astype(f32), axis=0)
    cross = total[:lanes]
    tail = total[lanes : lanes + NUMER + NS] + jnp.pad(total[lanes + NUMER + NS :], ((NUMER, 0), (0, 0)))
    mate = lax.ppermute(tail, "rows", swap)
    first = core == 0
    low = jnp.where(first, tail, mate)
    high = jnp.where(first, mate, tail)
    numer = jnp.concatenate([low[:NUMER], high[:NUMER]], axis=0)
    counts = jnp.concatenate([low[NUMER:], high[NUMER:]], axis=1)
    per_column = jnp.repeat(counts.T, SW, axis=1)
    new_codebook = (numer + codebook.astype(f32)) / (per_column + 1.0)
    return new_codebook, counts, cross


def solution(mesh):
    in_specs = (P(("rows", "feat"), None), P(None, "feat"), P(None, "feat"))
    out_specs = (P(None, "feat"), P("feat", None), P("rows", "feat"))
    return jax.shard_map(local, mesh=mesh, in_specs=in_specs, out_specs=out_specs, check_vma=False)
```

```python
import jax
import jax.numpy as jnp
from jax import lax
from jax.experimental import pallas as pl
from jax.experimental.pallas import tpu as pltpu
from jax.sharding import PartitionSpec as P

D = 1024
SUB = 64
K = 256
SW = D // SUB
W = 128
NS = W // SW
ROWS = 768
CHUNK = 256
CROSS = D // 2
NUMER = K // 2
HALF = CROSS + NUMER + NS
STEPS = (1, 2, 3, 4, 5, 6, 7, 0)
bf16 = jnp.bfloat16
f32 = jnp.float32


def dot(a, b, ca, cb):
    return lax.dot_general(a, b, (((ca,), (cb,)), ((), ())), preferred_element_type=f32)


def one_block(first, data_ref, mine, other, keep_ref, give_ref, codes_t, xaug, reb, wb, lhs_all):
    lo = jnp.where(first, mine[...], other[...])
    hi = jnp.where(first, other[...], mine[...])
    codes = jnp.concatenate([lo[CROSS:], hi[CROSS:]], axis=0)
    codes_t[...] = codes.astype(f32).T.astype(bf16)
    wide = codes.astype(f32)
    squares = wide * wide
    high = squares.astype(bf16)
    low = (squares - high.astype(f32)).astype(bf16)
    row_group = lax.broadcasted_iota(jnp.int32, (W, W), 0) // SW
    col_group = lax.broadcasted_iota(jnp.int32, (W, W), 1) // SW
    group_ones = jnp.where(row_group == col_group, 1.0, 0.0).astype(bf16)
    bias = -0.5 * (dot(high, group_ones, 1, 0) + dot(low, group_ones, 1, 0))
    lane = lax.broadcasted_iota(jnp.int32, (K, W), 1)
    b0 = bias.astype(bf16).astype(f32)
    b1 = (bias - b0).astype(bf16).astype(f32)
    b2 = bias - b0 - b1
    place = lane % SW
    aug = jnp.where(place == 0, b0, jnp.where(place == 1, b1, jnp.where(place == 2, b2, 0.0))).astype(bf16)
    rot = jnp.concatenate([lo[:CROSS], hi[:CROSS]], axis=0)
    xaug[0:W, :] = dot(rot, data_ref[...], 0, 0).astype(bf16)
    xaug[W:, :] = jnp.ones((W, ROWS), bf16)
    zero = jnp.zeros((K, W), bf16)
    for s in range(NS):
        mask = (lane // SW) == s
        lhs_all[s * K : (s + 1) * K, :] = jnp.concatenate(
            [jnp.where(mask, codes, zero), jnp.where(mask, aug, zero)], axis=1
        )
    for s in range(NS):
        for piece in range(ROWS // CHUNK):
            cols = slice(piece * CHUNK, (piece + 1) * CHUNK)
            logits = dot(lhs_all[s * K : (s + 1) * K, :], xaug[:, cols], 1, 0)
            e = jnp.exp(logits - jnp.max(logits, axis=0, keepdims=True))
            wb[s * K : (s + 1) * K, cols] = (e * (1.0 / jnp.sum(e, axis=0, keepdims=True))).astype(bf16)
    acc = jnp.zeros((K, 2 * W), f32)
    group2 = (lax.broadcasted_iota(jnp.int32, (K, 2 * W), 1) // SW) % NS
    for s in range(NS):
        own = slice(s * SW, (s + 1) * SW)
        weights = wb[s * K : (s + 1) * K, :]
        reb[own, :] = dot(codes_t[own, :], weights, 1, 0).astype(bf16)
        acc = jnp.where(group2 == s, dot(weights, xaug[...], 1, 1), acc)
    counts = acc[:, W:].T
    counts = jnp.concatenate([counts[s * SW : s * SW + 1] for s in range(NS)], axis=0)
    cross = dot(data_ref[...], reb[...], 1, 1)
    for ref, top in ((keep_ref, first), (give_ref, jnp.logical_not(first))):
        ref[:CROSS, :] = jnp.where(top, cross[:CROSS], cross[CROSS:])
        ref[CROSS : CROSS + NUMER, :] = jnp.where(top, acc[:NUMER, :W], acc[NUMER:, :W])
        ref[CROSS + NUMER :, :] = jnp.where(top, counts[:, :NUMER], counts[:, NUMER:])


def assign(core, data_t, packs):
    blocks = len(packs)

    def body(core_ref, data_ref, *refs):
        ins = refs[: 2 * blocks]
        outs = refs[2 * blocks : 4 * blocks]
        scratch = refs[4 * blocks :]
        first = core_ref[0] == 0
        for b in range(blocks):
            one_block(first, data_ref, ins[2 * b], ins[2 * b + 1], outs[2 * b], outs[2 * b + 1], *scratch)

    vmem = pl.BlockSpec(memory_space=pltpu.VMEM)
    flat = [half for pair in packs for half in pair]
    out = pl.pallas_call(
        body,
        in_specs=[pl.BlockSpec(memory_space=pltpu.SMEM), vmem] + [vmem] * len(flat),
        out_specs=[vmem] * (2 * blocks),
        out_shape=[jax.ShapeDtypeStruct((HALF, W), f32)] * (2 * blocks),
        scratch_shapes=[
            pltpu.VMEM((W, K), bf16),
            pltpu.VMEM((2 * W, ROWS), bf16),
            pltpu.VMEM((W, ROWS), bf16),
            pltpu.VMEM((NS * K, ROWS), bf16),
            pltpu.VMEM((NS * K, 2 * W), bf16),
        ],
        compiler_params=pltpu.CompilerParams(vmem_limit_bytes=24 * 1024 * 1024),
        cost_estimate=pl.CostEstimate(
            flops=blocks * 3_000_000_000, bytes_accessed=blocks * 4_000_000, transcendentals=blocks * NS * K * ROWS
        ),
        name="assign",
    )(core.reshape(1), data_t, *flat)
    return [(out[2 * b], out[2 * b + 1]) for b in range(blocks)]


def send(j, summed):
    n_feat = lax.axis_size("feat")
    return lax.ppermute(summed, "feat", [(i, (i + j) % n_feat) for i in range(n_feat)])


def local(data, rotation, codebook):
    n_feat = lax.axis_size("feat")
    n_rows = lax.axis_size("rows")
    pairs = n_rows // 2
    core = lax.axis_index("rows") % 2
    swap = [(i, i ^ 1) for i in range(n_rows)]
    lanes = D // n_rows
    by_core = rotation.reshape(pairs, 2, lanes, W)

    def part_of(h):
        rows = lax.dynamic_index_in_dim(by_core, h, axis=1, keepdims=False).reshape(CROSS, W)
        return jnp.concatenate([rows, lax.dynamic_slice_in_dim(codebook, h * NUMER, NUMER, axis=0)], axis=0)

    half = part_of(core)
    other_half = part_of(1 - core)
    data_t = data.reshape(ROWS, pairs, 2, lanes).transpose(2, 1, 3, 0).reshape(D, ROWS)
    packs = {0: (half, other_half)}
    for j in STEPS:
        if j:
            mine = lax.ppermute(half, "feat", [(i, (i - j) % n_feat) for i in range(n_feat)])
            packs[j] = (mine, lax.ppermute(mine, "rows", swap))
    waiting = []
    for j in STEPS:
        keep, give = assign(core, data_t, [packs[j]])[0]
        summed = keep + lax.ppermute(give, "rows", swap)
        if j:
            waiting.append((j, summed.astype(bf16)))
        else:
            own = summed
    part = None
    for j, summed in waiting:
        got = send(j, summed).astype(f32)
        part = got if part is None else part + got
    part = part + own
    n_x = 4
    n_z = pairs // n_x
    z_groups = [[x * 2 * n_z + z * 2 + c for z in range(n_z)] for x in range(n_x) for c in range(2)]
    x_groups = [[x * 2 * n_z + r for x in range(n_x)] for r in range(2 * n_z)]

    def stage(cross_part, rest, n, groups):
        rest_high = rest.astype(bf16)
        counts_low = (rest[NUMER:] - rest_high[NUMER:].astype(f32)).astype(bf16)
        all_rest = jnp.concatenate([rest_high, counts_low], axis=0)
        sent = jnp.concatenate(
            [cross_part.astype(bf16), jnp.broadcast_to(all_rest[None], (n,) + all_rest.shape)], axis=1
        )
        got = lax.all_to_all(sent, "rows", split_axis=0, concat_axis=0, tiled=True, axis_index_groups=groups)
        total = jnp.sum(got.astype(f32), axis=0)
        size = cross_part.shape[1]
        rest = total[size : size + NUMER + NS] + jnp.pad(total[size + NUMER + NS :], ((NUMER, 0), (0, 0)))
        return total[:size], rest

    by_z = part[:CROSS].reshape(n_x, n_z, lanes, W).transpose(1, 0, 2, 3).reshape(n_z, n_x * lanes, W)
    cross, tail = stage(by_z, part[CROSS:], n_z, z_groups)
    sent = jnp.concatenate(
        [cross.reshape(n_x, lanes, W), jnp.broadcast_to(tail[None], (n_x,) + tail.shape)], axis=1
    )
    total = jnp.sum(
        lax.all_to_all(sent, "rows", split_axis=0, concat_axis=0, tiled=True, axis_index_groups=x_groups), axis=0
    )
    cross = total[:lanes]
    tail = total[lanes:]
    mate = lax.ppermute(tail, "rows", swap)
    first = core == 0
    low = jnp.where(first, tail, mate)
    high = jnp.where(first, mate, tail)
    numer = jnp.concatenate([low[:NUMER], high[:NUMER]], axis=0)
    counts = jnp.concatenate([low[NUMER:], high[NUMER:]], axis=1)
    per_column = jnp.repeat(counts.T, SW, axis=1)
    new_codebook = (numer + codebook.astype(f32)) / (per_column + 1.0)
    return new_codebook, counts, cross


def solution(mesh):
    in_specs = (P(("rows", "feat"), None), P(None, "feat"), P(None, "feat"))
    out_specs = (P(None, "feat"), P("feat", None), P("rows", "feat"))
    return jax.shard_map(local, mesh=mesh, in_specs=in_specs, out_specs=out_specs, check_vma=False)
```
